32 devices in a mesh: groups: 2 (over x), expert: 4 (over y, core), tensor: 4 (over z).
Axes of the slice: x: 2, y: 2, z: 4, core: 2. Of those that a mesh axis runs over, the one named last changes fastest.
Arguments:
- tokens: bfloat16 [512, 2880], P(('groups', 'expert', 'tensor')), parts along dimension 0, may hold values from -6 to 6
- routes: int32 [512, 4], P(('groups', 'expert', 'tensor')), parts along dimension 0, may hold values from 0 to 15, all different within a row; in each aligned block of 16 rows (0 to 15, 16 to 31, ...) at most 8 rows name the same one
- route_weights: float32 [512, 4], P(('groups', 'expert', 'tensor')), parts along dimension 0, may hold values from 0.05 to 0.7
- w_gate_up: bfloat16 [16, 2880, 2, 2880], P('expert', None, None, 'tensor'), may hold values from -0.109375 to 0.109375
- bias_gate_up: float32 [16, 2, 2880], P('expert', None, 'tensor'), may hold values from -3 to 3
- w_down: bfloat16 [16, 2880, 2880], P('expert', 'tensor'), may hold values from -0.109375 to 0.109375
- down_bias: float32 [16, 2880], replicated, may hold values from -3 to 3
Outputs:
- moe_output: bfloat16 [512, 2880], P(('groups', 'expert', 'tensor')), parts along dimension 0
The draws below stay inside these ranges and needn't reach their ends.
There are 2 independent parts, one for each index of `groups`. The reference program is written for one: setup_inputs(seed, part) draws one part's arguments, and reference() takes and returns one part's arrays. A program takes and returns all parts, laid end to end along the dimension named above; an argument that names none is the same for every part. Nothing has to cross between parts.
Inputs may be any that keep to these rules, and one draw needn't show every extreme that they name: `routes`: each row names 4 different experts. In each aligned block of 16 rows (the rows of one device) no expert is named more than 8 times, a bound that some block reaches.
All inputs are finite; a program needn't handle non-finite values.
Results may differ from the reference program's by a relative error of at most 0.014.
Values may be sent and summed in bfloat16 or wider, within the bound.
A program may use at most 128 MiB of HBM per device.

```python
import math
import jax
import jax.numpy as jnp
import numpy as np
from jax import lax

D = 2880
FF = 2880
TOP = 4
EXPERTS = 16
TOK_DEV = 16
CAP = 8
TOKENS = 256
N_TENSOR = 4


def level_of(stream_key, shape, cuts, smallest, high):
    factor_of = 1.0
    for axis_at, blocks in cuts:
        heights = jax.random.uniform(jax.random.fold_in(jax.random.fold_in(stream_key, 6), axis_at), (blocks,), jnp.float32, smallest / len(cuts), high / len(cuts))
        factor_of = factor_of * jnp.repeat(jnp.exp(heights), shape[axis_at] // blocks).reshape((-1,) + (1,) * (len(shape) - 1 - axis_at))
    return factor_of


def shared_out(key, own, number, rows, number_of, top, most, lean):
    order = jax.random.permutation(key, number_of)
    packed, usual = shares(number_of, rows * top, most, lean, True), shares(number_of, rows * top, most, lean, False)
    places = jnp.arange(number_of)

    def named(tallies, turn):
        used = int((tallies > 0).sum())
        fixed = max(1, used // 4)
        passed = fixed + (places - fixed + turn * (used - fixed)) % max(1, number_of - fixed)
        return jnp.zeros((number_of,), jnp.int32).at[order[jnp.where(places < fixed, places, passed)]].set(jnp.asarray(tallies, jnp.int32))

    tallies = jnp.where(number % 4 == 0, named(packed, number // 4), named(usual, number - number // 4 - 1))
    mixed = jax.random.permutation(jax.random.fold_in(own, 3), number_of)
    source_of, taker = mixed[0:number_of // 2 * 2:2], mixed[1:number_of // 2 * 2:2]
    margin = jnp.minimum(tallies[source_of] - 1, most - tallies[taker]) // 2
    margin = jnp.where((source_of == order[0]) | (taker == order[0]) | (tallies[taker] == 0), 0, jnp.maximum(margin, 0))
    passed = jax.random.randint(jax.random.fold_in(own, 4), (number_of // 2,), 0, 1 << 20) % (margin + 1)
    tallies = tallies.at[source_of].add(-passed).at[taker].add(passed)
    items = jnp.searchsorted(jnp.cumsum(tallies), jnp.arange(rows * top), side="right").astype(jnp.int32)
    table = items.reshape(top, rows).T
    table = table[jax.random.permutation(jax.random.fold_in(own, 1), rows)]
    turn = jax.random.randint(jax.random.fold_in(own, 2), (rows, 1), 0, top)
    return jnp.take_along_axis(table, (jnp.arange(top)[None, :] + turn) % top, axis=1)


def shares(count, total, bound, slope, full):
    weights = [(1 << 20) // math.isqrt(standing ** slope) + 1 for standing in range(1, count + 1)]
    largest = bound if full else min(bound, max(-(-total // count), total * weights[0] // sum(weights)))
    least = 1 if total - largest >= count - 1 else 0
    counts, surplus = [largest] + [least] * (count - 1), total - largest - least * (count - 1)
    while surplus > 0:
        movable = [i for i in range(1, count) if counts[i] < largest] or [i for i in range(1, count) if counts[i] < bound]
        whole, budget = sum([weights[i] for i in movable]), surplus
        for i in movable:
            more = min(bound - counts[i], max(1, budget * weights[i] // whole), surplus)
            counts[i] = counts[i] + more
            surplus = surplus - more
    return np.array(counts)


def gaussian(rng, extent, spread, bound, shards=(), kind=jnp.bfloat16):
    factor_of = level_of(rng, extent, shards, -0.22, 0.18) if shards else 1.0
    values = jax.random.normal(rng, extent, jnp.float32) * spread * factor_of
    return jnp.minimum(jnp.maximum(values, -bound), bound).astype(kind)


def setup_inputs(seed: int = 0, part: int = 0) -> dict:
    arg_keys = jax.random.split(jax.random.key(seed), 8)
    part_keys = jax.random.split(jax.random.fold_in(arg_keys[7], part), 8)
    tokens = gaussian(part_keys[0], (TOKENS, D), 1.0, 6.0, ((0, 16),))
    routes_keys = jax.random.split(jax.random.fold_in(part_keys[1], 1), TOKENS // TOK_DEV)
    routes_turns = jax.random.permutation(jax.random.fold_in(part_keys[1], 3), TOKENS // TOK_DEV)
    routes = jax.vmap(lambda own, number: shared_out(jax.random.fold_in(part_keys[1], 2), own, number, TOK_DEV, EXPERTS, TOP, CAP, 2))(routes_keys, routes_turns).reshape((TOKENS, TOP))
    route_weights = jnp.clip(jnp.exp(math.log(0.7) - 2.6390573 * jax.random.uniform(part_keys[2], (TOKENS, TOP), jnp.float32) ** level_of(part_keys[2], (TOKENS, TOP), ((0, 16),), -0.2, 0.2)), 0.05, 0.7)
    w_gate_up = gaussian(arg_keys[3], (EXPERTS, D, 2, FF), D ** -0.5, 0.109375, ((0, 4), (3, 4)))
    bias_gate_up = gaussian(arg_keys[4], (EXPERTS, 2, FF), 0.5, 3.0, ((0, 4), (2, 4)), jnp.float32)
    w_down = gaussian(arg_keys[5], (EXPERTS, FF, D), FF ** -0.5, 0.109375, ((0, 4), (1, 4)))
    down_bias = gaussian(arg_keys[6], (EXPERTS, D), 0.5, 3.0, (), jnp.float32)
    return dict(tokens=tokens, routes=routes, route_weights=route_weights, w_gate_up=w_gate_up, bias_gate_up=bias_gate_up, w_down=w_down, down_bias=down_bias)


def slot_index(route_block):
    flat_routes = route_block.reshape(-1)
    hit_table = (flat_routes[:, None] == jnp.arange(EXPERTS, dtype=jnp.int32)[None, :]).astype(jnp.int32)
    before = jnp.cumsum(hit_table, axis=0) - hit_table
    slot = jnp.sum(before * hit_table, axis=1)
    return (flat_routes * CAP + slot).astype(jnp.int32)


def reference(tokens, routes, route_weights, w_gate_up, bias_gate_up, w_down, down_bias):
    blocks = TOKENS // TOK_DEV
    slot_total = EXPERTS * CAP
    tok_blocks = tokens.reshape(blocks, TOK_DEV, D)
    targets = jax.vmap(slot_index)(routes.reshape(blocks, TOK_DEV, TOP))

    def fill_block(tok_block, dst_block):
        empty = jnp.zeros((slot_total, D), jnp.bfloat16)
        return empty.at[dst_block].set(jnp.repeat(tok_block, TOP, axis=0))

    buffers = jax.vmap(fill_block)(tok_blocks, targets).reshape(blocks, EXPERTS, CAP, D)
    group = FF // N_TENSOR

    def expert(expert_id):
        row_block = buffers[:, expert_id].reshape(blocks * CAP, D)
        w_joined = w_gate_up[expert_id].reshape(D, 2 * FF)
        projected = jnp.dot(row_block, w_joined, preferred_element_type=jnp.float32)
        projected = projected + bias_gate_up[expert_id].reshape(2 * FF)[None, :]
        gate_part = projected[:, :FF]
        up_part = projected[:, FF:]
        hidden = (gate_part * jax.nn.sigmoid(1.702 * gate_part) * (up_part + 1.0)).astype(jnp.bfloat16)
        hidden_groups = hidden.reshape(blocks * CAP, N_TENSOR, group).astype(jnp.float32)
        down_groups = w_down[expert_id].reshape(N_TENSOR, group, D).astype(jnp.float32)
        partials = jnp.einsum('rnf,nfd->nrd', hidden_groups, down_groups).astype(jnp.bfloat16)
        summed = jnp.sum(partials.astype(jnp.float32), axis=0) + down_bias[expert_id][None, :]
        return summed.astype(jnp.bfloat16).reshape(blocks, CAP, D)

    expert_outs = lax.map(expert, jnp.arange(EXPERTS, dtype=jnp.int32))
    slot_table = jnp.swapaxes(expert_outs, 0, 1).reshape(blocks, slot_total, D)

    def pick_rows(slot_rows, index_rows):
        return slot_rows[index_rows]

    picked = jax.vmap(pick_rows)(slot_table, targets).astype(jnp.float32).reshape(TOKENS, TOP, D)
    combined = jnp.sum(picked * route_weights[:, :, None], axis=1)
    return combined.astype(jnp.bfloat16)
```

```python
import functools

import jax
import jax.numpy as jnp
from jax import lax
from jax.experimental import pallas as pl
from jax.experimental.pallas import tpu as pltpu
from jax.sharding import PartitionSpec as P

TOP = 4
EXPERTS = 16
CAP = 8


def activate(projected, half_width):
    gate_part = projected[..., :half_width]
    up_part = projected[..., half_width:]
    return (gate_part * jax.nn.sigmoid(1.702 * gate_part) * (up_part + 1.0)).astype(jnp.bfloat16)


def local(tokens, routes, route_weights, w_gate_up, bias_gate_up, w_down, down_bias):
    tok_rows, model_width = tokens.shape
    n_expert = lax.axis_size("expert")
    local_count = EXPERTS // n_expert
    slot_total = EXPERTS * CAP
    half_width = w_gate_up.shape[3]
    flat_routes = routes.reshape(-1)
    hit_table = (flat_routes[:, None] == jnp.arange(EXPERTS, dtype=jnp.int32)[None, :]).astype(
        jnp.int32
    )
    before = jnp.cumsum(hit_table, axis=0) - hit_table
    slot = jnp.sum(before * hit_table, axis=1)
    target = (flat_routes * CAP + slot).reshape(tok_rows, TOP)
    choose = target[:, :, None] == jnp.arange(slot_total, dtype=jnp.int32)[None, None, :]
    pick_table = jnp.sum(choose, axis=1).astype(jnp.bfloat16)
    outgoing = jnp.einsum("ts,td->sd", pick_table, tokens, preferred_element_type=jnp.float32)
    outgoing = outgoing.astype(jnp.bfloat16).reshape(n_expert, local_count, CAP, model_width)
    w_joined = w_gate_up.reshape(local_count, model_width, 2 * half_width)
    bias_joined = bias_gate_up.reshape(local_count, 2 * half_width)
    received = lax.all_to_all(outgoing, "expert", split_axis=0, concat_axis=0, tiled=True)
    projected = jnp.einsum(
        "...lcd,ldf->...lcf",
        lax.all_gather(received, "tensor", axis=0, tiled=True),
        w_joined,
        preferred_element_type=jnp.float32,
    )
    hidden = activate(projected + bias_joined[:, None, :], half_width)
    summed = lax.psum_scatter(
        jnp.einsum("rlcf,lfd->rlcd", hidden, w_down, preferred_element_type=jnp.float32).astype(
            jnp.bfloat16
        ),
        "tensor",
        scatter_dimension=0,
        tiled=True,
    ).astype(jnp.float32)
    own_bias = lax.dynamic_slice_in_dim(
        down_bias, lax.axis_index("expert") * local_count, local_count, 0
    )
    result = (summed + own_bias[None, :, None, :]).astype(jnp.bfloat16)
    back = lax.all_to_all(result, "expert", split_axis=0, concat_axis=0, tiled=True)
    slot_table = back.reshape(slot_total, model_width).astype(jnp.float32)
    weighted = jnp.sum(route_weights[:, :, None] * choose.astype(jnp.float32), axis=1)
    combined = jnp.dot(weighted, slot_table, precision=lax.Precision.HIGHEST)
    return combined.astype(jnp.bfloat16)


MESH = pl.DeviceIdType.MESH


def fused(widths, tok_ref, route_ref, weight_ref, bias_ref, down_bias_ref, wg_hbm, wd_hbm, out_ref, *scratch):
    (wg, wd, xs, xt, ht, hid, bias_t, keep, base, ag_send, ag_recv, rs_send, rs_recv, w_sem) = scratch[:14]
    chunks = len(widths)
    send1, recv1, send2, recv2, send3, recv3 = (
        scratch[14 + i * chunks : 14 + (i + 1) * chunks] for i in range(6)
    )
    count, _, half_width, model = wg_hbm.shape
    rows = tok_ref.shape[0]
    g, e, t = lax.axis_index("groups"), lax.axis_index("expert"), lax.axis_index("tensor")
    core_peer = (g, e + 1 - 2 * (e % 2), t)
    y_peer = (g, (e + 2) % 4, t)
    z_peers = (
        None,
        (g, e, t + 1 - 2 * (t % 2)),
        (g, e, (t + 2) % 4),
        (g, e, 3 - t),
    )
    partners = (core_peer, y_peer, z_peers[1], z_peers[2], z_peers[3])

    barrier = pltpu.get_barrier_semaphore()
    for partner in partners:
        pl.semaphore_signal(barrier, inc=1, device_id=partner, device_id_type=MESH)

    loads = []
    for l in range(count):
        loads.append(pltpu.make_async_copy(wg_hbm.at[l], wg.at[l], w_sem.at[l]))
    for l in range(count):
        loads.append(
            pltpu.make_async_copy(
                wd_hbm.at[l], wd.at[pl.ds(l * half_width, half_width)], w_sem.at[count + l]
            )
        )
    for load in loads:
        load.start()

    expert_at = lax.broadcasted_iota(jnp.int32, (128, rows), 0)
    table_t = jnp.zeros((128, rows), jnp.float32)
    for k in range(TOP):
        table_t += jnp.where(
            expert_at % EXPERTS == route_ref[k : k + 1, :], weight_ref[k : k + 1, :], 0.0
        )
    table = jnp.transpose(
        jnp.concatenate([table_t, jnp.zeros((128, 128 - rows), jnp.float32)], axis=1)
    )[:rows]
    high = table.astype(jnp.bfloat16).astype(jnp.float32)
    lane = lax.broadcasted_iota(jnp.int32, (rows, 128), 1)
    coded = jnp.where(lane < EXPERTS, high, jnp.where(lane < 2 * EXPERTS, table - high, 0.0))
    wide = xs.shape[2]
    xs[0, :, :model] = tok_ref[...]
    xs[0, :, wide - 128 :] = coded.astype(jnp.bfloat16)

    pl.semaphore_wait(barrier, len(partners))

    def hop(index, source, target, peer):
        return pltpu.make_async_remote_copy(
            src_ref=xs.at[source],
            dst_ref=xs.at[target],
            send_sem=ag_send.at[index],
            recv_sem=ag_recv.at[index],
            device_id=peer,
            device_id_type=MESH,
        )

    z_hop = [None] + [hop(j - 1, 0, j, z_peers[j]) for j in (1, 2, 3)]
    y_hop = [hop(3 + j, j, 4 + j, y_peer) for j in range(4)]
    c_hop = [hop(7 + s, s, 8 + s, core_peer) for s in range(8)]
    y_hop[0].start()
    z_hop[3].start()
    z_hop[2].start()
    z_hop[1].start()
    c_hop[0].start()

    own = table[:, 0:1] * down_bias_ref[0:1, :]
    for k in range(1, EXPERTS):
        own += table[:, k : k + 1] * down_bias_ref[k : k + 1, :]
    base[...] = own
    bias_t[...] = jnp.transpose(bias_ref[...])

    for j in (1, 2, 3):
        z_hop[j].wait_recv()
        y_hop[j].start()
        c_hop[j].start()
        y_hop[j - 1].wait_recv()
        c_hop[4 + j - 1].start()
    y_hop[3].wait_recv()
    c_hop[7].start()
    for s in range(8):
        c_hop[s].wait_recv()

    everything = xs[...].reshape(16 * rows, wide)
    xt[...] = jnp.transpose(everything[:, :model])
    spread = everything[:, wide - 128 :]
    row_at = lax.broadcasted_iota(jnp.int32, (16, 128), 0)
    lane_at = lax.broadcasted_iota(jnp.int32, (16, 128), 1)
    select = jnp.where(
        (lane_at % EXPERTS == row_at + e * count) & (lane_at < 2 * EXPERTS) & (row_at < count), 1.0, 0.0
    ).astype(jnp.bfloat16)
    shares = lax.dot_general(
        select, spread, (((1,), (1,)), ((), ())), preferred_element_type=jnp.float32
    )

    for l in range(count):
        loads[l].wait()
        gate = jnp.dot(wg[l, 0], xt[...], preferred_element_type=jnp.float32)
        gate = gate + bias_t[:, 2 * l : 2 * l + 1]
        up = jnp.dot(wg[l, 1], xt[...], preferred_element_type=jnp.float32)
        up = up + bias_t[:, 2 * l + 1 : 2 * l + 2]
        hidden = gate * jax.nn.sigmoid(1.702 * gate) * (up + 1.0) * shares[l : l + 1, :]
        ht[l * half_width : (l + 1) * half_width, :] = hidden.astype(jnp.bfloat16)
    hid[...] = jnp.transpose(ht[...])
    for l in range(count):
        loads[count + l].wait()

    starts = [sum(widths[:c]) for c in range(chunks)]

    def rs_hop(c, index, source, target, peer):
        return pltpu.make_async_remote_copy(
            src_ref=source,
            dst_ref=target,
            send_sem=rs_send.at[c * 5 + index],
            recv_sem=rs_recv.at[c * 5 + index],
            device_id=peer,
            device_id_type=MESH,
        )

    hop1 = [rs_hop(c, 0, send1[c], recv1[c], core_peer) for c in range(chunks)]
    hop2 = [rs_hop(c, 1, send2[c], recv2[c], y_peer) for c in range(chunks)]
    hop3 = [
        [
            rs_hop(c, 1 + j, send3[c].at[j - 1], recv3[c].at[j - 1], z_peers[j])
            for j in (1, 2, 3)
        ]
        for c in range(chunks)
    ]

    def stage1(c):
        at, width = starts[c], widths[c]
        part = jnp.dot(
            hid[...], wd[:, at : at + width], preferred_element_type=jnp.float32
        )
        send1[c][...] = part[8 * rows :].astype(jnp.bfloat16)
        hop1[c].start()
        keep[:, at : at + width] = part[: 8 * rows]

    def stage2(c):
        at, width = starts[c], widths[c]
        hop1[c].wait_recv()
        send2[c][...] = (
            keep[4 * rows :, at : at + width] + recv1[c][4 * rows :].astype(jnp.float32)
        ).astype(jnp.bfloat16)
        hop2[c].start()
        keep[: 4 * rows, at : at + width] = keep[: 4 * rows, at : at + width] + recv1[c][
            : 4 * rows
        ].astype(jnp.float32)

    def stage3(c):
        at, width = starts[c], widths[c]
        hop2[c].wait_recv()
        for j in (3, 2, 1):
            band = slice(j * rows, (j + 1) * rows)
            send3[c][j - 1] = (
                keep[band, at : at + width] + recv2[c][band].astype(jnp.float32)
            ).astype(jnp.bfloat16)
            hop3[c][j - 1].start()
        keep[:rows, at : at + width] = keep[:rows, at : at + width] + recv2[c][:rows].astype(
            jnp.float32
        )

    def stage4(c):
        at, width = starts[c], widths[c]
        total = keep[:rows, at : at + width] + base[:, at : at + width]
        for j in (1, 2, 3):
            hop3[c][j - 1].wait_recv()
            total += recv3[c][j - 1].astype(jnp.float32)
        out_ref[:, at : at + width] = total.astype(jnp.bfloat16)

    for step in range(chunks + 3):
        for lag, stage in enumerate((stage1, stage2, stage3, stage4)):
            if 0 <= step - lag < chunks:
                stage(step - lag)

    for copy in z_hop[1:] + y_hop + c_hop + hop1 + hop2 + sum(hop3, []):
        copy.wait_send()


def fused_local(tokens, routes, route_weights, w_gate_up, bias_gate_up, w_down, down_bias):
    rows, model = tokens.shape
    count, _, _, half_width = w_gate_up.shape
    widths = []
    while sum(widths) < model:
        widths.append(min(768, model - sum(widths)))
    wide = -(-model // 128) * 128 + 128
    total = 16 * rows
    bf16, f32 = jnp.bfloat16, jnp.float32
    scratch = [
        pltpu.VMEM((count, 2, half_width, model), bf16),
        pltpu.VMEM((count * half_width, model), bf16),
        pltpu.VMEM((16, rows, wide), bf16),
        pltpu.VMEM((model, total), bf16),
        pltpu.VMEM((count * half_width, total), bf16),
        pltpu.VMEM((total, count * half_width), bf16),
        pltpu.VMEM((half_width, 2 * count), f32),
        pltpu.VMEM((8 * rows, model), f32),
        pltpu.VMEM((rows, model), f32),
        pltpu.SemaphoreType.DMA((15,)),
        pltpu.SemaphoreType.DMA((15,)),
        pltpu.SemaphoreType.DMA((5 * len(widths),)),
        pltpu.SemaphoreType.DMA((5 * len(widths),)),
        pltpu.SemaphoreType.DMA((2 * count,)),
    ]
    for shape in ((8 * rows,), (4 * rows,), (3, rows)):
        for _ in range(2):
            scratch += [pltpu.VMEM(shape + (w,), bf16) for w in widths]
    in_vmem = pl.BlockSpec(memory_space=pltpu.VMEM)
    return pl.pallas_call(
        functools.partial(fused, tuple(widths)),
        out_shape=jax.ShapeDtypeStruct((rows, model), bf16),
        in_specs=[in_vmem] * 5 + [pl.BlockSpec(memory_space=pl.ANY)] * 2,
        out_specs=in_vmem,
        scratch_shapes=scratch,
        compiler_params=pltpu.CompilerParams(
            collective_id=0, has_side_effects=True, vmem_limit_bytes=63 * 1024 * 1024
        ),
        cost_estimate=pl.CostEstimate(
            flops=6 * total * count * half_width * model,
            bytes_accessed=6 * count * half_width * model,
            transcendentals=total * count * half_width,
        ),
    )(
        tokens,
        jnp.transpose(routes),
        jnp.transpose(route_weights),
        bias_gate_up.reshape(2 * count, half_width),
        down_bias,
        jnp.transpose(w_gate_up, (0, 2, 3, 1)),
        w_down,
    )


def solution(mesh):
    small = mesh.shape["expert"] == 4 and mesh.shape["tensor"] == 4
    return jax.shard_map(
        fused_local if small else local,
        mesh=mesh,
        in_specs=(
            P(("groups", "expert", "tensor"), None),
            P(("groups", "expert", "tensor"), None),
            P(("groups", "expert", "tensor"), None),
            P("expert", None, None, "tensor"),
            P("expert", None, "tensor"),
            P("expert", "tensor", None),
            P(),
        ),
        out_specs=P(("groups", "expert", "tensor"), None),
        check_vma=False,
    )
```

```python
import functools

import jax
import jax.numpy as jnp
from jax import lax
from jax.experimental import pallas as pl
from jax.experimental.pallas import tpu as pltpu
from jax.sharding import PartitionSpec as P

TOP = 4
EXPERTS = 16
CAP = 8


def activate(projected, half_width):
    gate_part = projected[..., :half_width]
    up_part = projected[..., half_width:]
    return (gate_part * jax.nn.sigmoid(1.702 * gate_part) * (up_part + 1.0)).astype(jnp.bfloat16)


def local(tokens, routes, route_weights, w_gate_up, bias_gate_up, w_down, down_bias):
    tok_rows, model_width = tokens.shape
    n_expert = lax.axis_size("expert")
    local_count = EXPERTS // n_expert
    slot_total = EXPERTS * CAP
    half_width = w_gate_up.shape[3]
    flat_routes = routes.reshape(-1)
    hit_table = (flat_routes[:, None] == jnp.arange(EXPERTS, dtype=jnp.int32)[None, :]).astype(
        jnp.int32
    )
    before = jnp.cumsum(hit_table, axis=0) - hit_table
    slot = jnp.sum(before * hit_table, axis=1)
    target = (flat_routes * CAP + slot).reshape(tok_rows, TOP)
    choose = target[:, :, None] == jnp.arange(slot_total, dtype=jnp.int32)[None, None, :]
    pick_table = jnp.sum(choose, axis=1).astype(jnp.bfloat16)
    outgoing = jnp.einsum("ts,td->sd", pick_table, tokens, preferred_element_type=jnp.float32)
    outgoing = outgoing.astype(jnp.bfloat16).reshape(n_expert, local_count, CAP, model_width)
    w_joined = w_gate_up.reshape(local_count, model_width, 2 * half_width)
    bias_joined = bias_gate_up.reshape(local_count, 2 * half_width)
    received = lax.all_to_all(outgoing, "expert", split_axis=0, concat_axis=0, tiled=True)
    projected = jnp.einsum(
        "...lcd,ldf->...lcf",
        lax.all_gather(received, "tensor", axis=0, tiled=True),
        w_joined,
        preferred_element_type=jnp.float32,
    )
    hidden = activate(projected + bias_joined[:, None, :], half_width)
    summed = lax.psum_scatter(
        jnp.einsum("rlcf,lfd->rlcd", hidden, w_down, preferred_element_type=jnp.float32).astype(
            jnp.bfloat16
        ),
        "tensor",
        scatter_dimension=0,
        tiled=True,
    ).astype(jnp.float32)
    own_bias = lax.dynamic_slice_in_dim(
        down_bias, lax.axis_index("expert") * local_count, local_count, 0
    )
    result = (summed + own_bias[None, :, None, :]).astype(jnp.bfloat16)
    back = lax.all_to_all(result, "expert", split_axis=0, concat_axis=0, tiled=True)
    slot_table = back.reshape(slot_total, model_width).astype(jnp.float32)
    weighted = jnp.sum(route_weights[:, :, None] * choose.astype(jnp.float32), axis=1)
    combined = jnp.dot(weighted, slot_table, precision=lax.Precision.HIGHEST)
    return combined.astype(jnp.bfloat16)


MESH = pl.DeviceIdType.MESH


def fused(widths, tok_ref, route_ref, weight_ref, bias_ref, down_bias_ref, wg_hbm, wd_hbm, out_ref, *scratch):
    (wg, wd, xa, xb, xta, xtb, acc, hid, bias_t, keep, base, ag_send, ag_recv, rs_send, rs_recv, w_sem) = scratch[:16]
    chunks = len(widths)
    send1, recv1, send2, recv2, send3, recv3 = (
        scratch[16 + i * chunks : 16 + (i + 1) * chunks] for i in range(6)
    )
    count, _, half_width, model = wg_hbm.shape
    rows = tok_ref.shape[0]
    g, e, t = lax.axis_index("groups"), lax.axis_index("expert"), lax.axis_index("tensor")
    core_peer = (g, e + 1 - 2 * (e % 2), t)
    y_peer = (g, (e + 2) % 4, t)
    z_near, z_far = (g, e, t + 1 - 2 * (t % 2)), (g, e, (t + 2) % 4)
    partners = (core_peer, y_peer, z_near, z_far)

    barrier = pltpu.get_barrier_semaphore()
    for partner in partners:
        pl.semaphore_signal(barrier, inc=1, device_id=partner, device_id_type=MESH)

    loads = []
    for l in range(count):
        loads.append(pltpu.make_async_copy(wg_hbm.at[l], wg.at[l], w_sem.at[l]))
    for l in range(count):
        loads.append(
            pltpu.make_async_copy(
                wd_hbm.at[l], wd.at[pl.ds(l * half_width, half_width)], w_sem.at[count + l]
            )
        )
    for load in loads:
        load.start()

    expert_at = lax.broadcasted_iota(jnp.int32, (128, rows), 0)
    table_t = jnp.zeros((128, rows), jnp.float32)
    for k in range(TOP):
        table_t += jnp.where(
            expert_at % EXPERTS == route_ref[k : k + 1, :], weight_ref[k : k + 1, :], 0.0
        )
    table = jnp.transpose(
        jnp.concatenate([table_t, jnp.zeros((128, 128 - rows), jnp.float32)], axis=1)
    )[:rows]
    high = table.astype(jnp.bfloat16).astype(jnp.float32)
    lane = lax.broadcasted_iota(jnp.int32, (rows, 128), 1)
    coded = jnp.where(lane < EXPERTS, high, jnp.where(lane < 2 * EXPERTS, table - high, 0.0))
    xs = (xa, xb)
    cut, rest = xa.shape[2], model - xa.shape[2]
    spare = xb.shape[2] - rest
    xa[0] = tok_ref[:, :cut]
    xb[0] = jnp.concatenate([tok_ref[:, cut:], coded[:, :spare].astype(jnp.bfloat16)], axis=1)

    pl.semaphore_wait(barrier, len(partners))

    def hop(half, index, source, target, peer):
        return pltpu.make_async_remote_copy(
            src_ref=xs[half].at[source],
            dst_ref=xs[half].at[target],
            send_sem=ag_send.at[half * 14 + index],
            recv_sem=ag_recv.at[half * 14 + index],
            device_id=peer,
            device_id_type=MESH,
        )

    z_hop = [
        [None, hop(h, 0, 0, 1, z_near), hop(h, 1, 0, 2, z_far), hop(h, 2, 2, 3, z_near)]
        for h in (0, 1)
    ]
    y_hop = [[hop(h, 3 + j, j, 4 + j, y_peer) for j in range(4)] for h in (0, 1)]
    c_hop = [[hop(h, 7 + s, s, 8 + s, core_peer) for s in range(7)] for h in (0, 1)]
    for h in (0, 1):
        c_hop[h].append(
            pltpu.make_async_remote_copy(
                src_ref=xs[h].at[7],
                dst_ref=xs[h].at[15],
                send_sem=ag_send.at[28 + h],
                recv_sem=ag_recv.at[28 + h],
                device_id=core_peer,
                device_id_type=MESH,
            )
        )
    for h in (0, 1):
        y_hop[h][0].start()
        z_hop[h][1].start()
        z_hop[h][2].start()
        c_hop[h][0].start()

    own = table[:, 0:1] * down_bias_ref[0:1, :]
    for k in range(1, EXPERTS):
        own += table[:, k : k + 1] * down_bias_ref[k : k + 1, :]
    base[...] = own
    bias_t[...] = jnp.transpose(jnp.concatenate([bias_ref[l] for l in range(count)], axis=0))

    def z_in(h, j):
        z_hop[h][j].wait_recv()
        if j == 2:
            z_hop[h][3].start()
        y_hop[h][j].start()
        c_hop[h][j].start()

    def y_in(h, j):
        y_hop[h][j].wait_recv()
        c_hop[h][4 + j].start()

    def all_in(h):
        for s in range(8):
            c_hop[h][s].wait_recv()

    z_in(0, 1)
    y_in(0, 0)
    z_in(0, 2)
    y_in(1, 0)
    z_in(1, 1)
    y_in(0, 1)
    z_in(1, 2)
    z_in(0, 3)
    y_in(0, 2)
    y_in(1, 1)
    z_in(1, 3)
    y_in(1, 2)
    y_in(0, 3)
    all_in(0)
    xta[...] = jnp.transpose(xa[...].reshape(16 * rows, cut))

    def first_half(l, part):
        return jnp.dot(wg[l, part, :, :cut], xta[...], preferred_element_type=jnp.float32)

    early = acc.shape[0]
    for l in range(early):
        loads[l].wait()
        for part in (0, 1):
            acc[l, part] = first_half(l, part)
        if l == 0:
            y_in(1, 3)
    all_in(1)

    everything = xb[...].reshape(16 * rows, rest + spare)
    xtb[...] = jnp.transpose(everything[:, :rest])
    spread = everything[:, rest:]
    row_at = lax.broadcasted_iota(jnp.int32, (16, spare), 0)
    lane_at = lax.broadcasted_iota(jnp.int32, (16, spare), 1)
    select = jnp.where(
        (lane_at % EXPERTS == row_at + e * count) & (lane_at < 2 * EXPERTS) & (row_at < count), 1.0, 0.0
    ).astype(jnp.bfloat16)
    shares = lax.dot_general(
        select, spread, (((1,), (1,)), ((), ())), preferred_element_type=jnp.float32
    )

    for l in range(count):
        if l >= early:
            loads[l].wait()
        gate, up = (
            (acc[l, part] if l < early else first_half(l, part))
            + jnp.dot(wg[l, part, :, cut:], xtb[...], preferred_element_type=jnp.float32)
            + bias_t[:, 2 * l + part : 2 * l + part + 1]
            for part in (0, 1)
        )
        hidden = gate * jax.nn.sigmoid(1.702 * gate) * (up + 1.0) * shares[l : l + 1, :]
        hid[:, l * half_width : (l + 1) * half_width] = jnp.transpose(
            hidden.astype(jnp.bfloat16)
        )
    for l in range(count):
        loads[count + l].wait()

    starts = [sum(widths[:c]) for c in range(chunks)]

    def rs_hop(c, index, source, target, peer):
        return pltpu.make_async_remote_copy(
            src_ref=source,
            dst_ref=target,
            send_sem=rs_send.at[c * 5 + index],
            recv_sem=rs_recv.at[c * 5 + index],
            device_id=peer,
            device_id_type=MESH,
        )

    hop1 = [rs_hop(c, 0, send1[c], recv1[c], core_peer) for c in range(chunks)]
    hop2 = [rs_hop(c, 1, send2[c], recv2[c], y_peer) for c in range(chunks)]
    hop3 = [
        [
            rs_hop(c, 1 + j, send3[c].at[j - 1], recv3[c].at[j - 1], z_far if j == 2 else z_near)
            for j in (1, 2, 3)
        ]
        for c in range(chunks)
    ]

    def stage1(c):
        at, width = starts[c], widths[c]
        part = jnp.dot(
            hid[...], wd[:, at : at + width], preferred_element_type=jnp.float32
        )
        send1[c][...] = part[8 * rows :].astype(jnp.bfloat16)
        hop1[c].start()
        keep[:, at : at + width] = part[: 8 * rows]

    def stage2(c):
        at, width = starts[c], widths[c]
        hop1[c].wait_recv()
        send2[c][...] = (
            keep[4 * rows :, at : at + width] + recv1[c][4 * rows :].astype(jnp.float32)
        ).astype(jnp.bfloat16)
        hop2[c].start()
        keep[: 4 * rows, at : at + width] = keep[: 4 * rows, at : at + width] + recv1[c][
            : 4 * rows
        ].astype(jnp.float32)

    def stage3(c):
        at, width = starts[c], widths[c]
        hop2[c].wait_recv()
        for j in (3, 1):
            band = slice(j * rows, (j + 1) * rows)
            send3[c][j - 1] = (
                keep[band, at : at + width] + recv2[c][band].astype(jnp.float32)
            ).astype(jnp.bfloat16)
            hop3[c][j - 1].start()

    def stage4(c):
        at, width = starts[c], widths[c]
        band = slice(2 * rows, 3 * rows)
        both = keep[band, at : at + width] + recv2[c][band].astype(jnp.float32)
        hop3[c][2].wait_recv()
        send3[c][1] = (both + recv3[c][2].astype(jnp.float32)).astype(jnp.bfloat16)
        hop3[c][1].start()

    def stage5(c):
        at, width = starts[c], widths[c]
        total = keep[:rows, at : at + width] + base[:, at : at + width]
        total += recv2[c][:rows].astype(jnp.float32)
        for j in (1, 2):
            hop3[c][j - 1].wait_recv()
            total += recv3[c][j - 1].astype(jnp.float32)
        out_ref[:, at : at + width] = total.astype(jnp.bfloat16)

    for step in range(chunks + 1):
        if step < chunks:
            stage1(step)
        if step >= 1:
            stage2(step - 1)
    for step in range(chunks + 2):
        if step < chunks:
            stage3(step)
        if step >= 2:
            stage4(step - 2)
    for c in range(chunks):
        stage5(c)

    ag_hops = [copy for h in (0, 1) for copy in z_hop[h][1:] + y_hop[h] + c_hop[h]]
    for copy in ag_hops + hop1 + hop2 + sum(hop3, []):
        copy.wait_send()


def fused_local(tokens, routes, route_weights, w_gate_up, bias_gate_up, w_down, down_bias):
    rows, model = tokens.shape
    count, _, _, half_width = w_gate_up.shape
    widths = []
    while sum(widths) < model:
        widths.append(min(512, model - sum(widths)))
    wide = -(-(model + 2 * EXPERTS) // 128) * 128
    cut = wide // 512 * 256 + 256
    total = 16 * rows
    bf16, f32 = jnp.bfloat16, jnp.float32
    scratch = [
        pltpu.VMEM((count, 2, half_width, model), bf16),
        pltpu.VMEM((count * half_width, model), bf16),
        pltpu.VMEM((16, rows, cut), bf16),
        pltpu.VMEM((16, rows, wide - cut), bf16),
        pltpu.VMEM((cut, total), bf16),
        pltpu.VMEM((model - cut, total), bf16),
        pltpu.VMEM((2, 2, half_width, total), f32),
        pltpu.VMEM((total, count * half_width), bf16),
        pltpu.VMEM((half_width, 2 * count), f32),
        pltpu.VMEM((8 * rows, model), f32),
        pltpu.VMEM((rows, model), f32),
        pltpu.SemaphoreType.DMA((30,)),
        pltpu.SemaphoreType.DMA((30,)),
        pltpu.SemaphoreType.DMA((5 * len(widths),)),
        pltpu.SemaphoreType.DMA((5 * len(widths),)),
        pltpu.SemaphoreType.DMA((2 * count,)),
    ]
    for shape in ((8 * rows,), (4 * rows,), (3, rows)):
        for _ in range(2):
            scratch += [pltpu.VMEM(shape + (w,), bf16) for w in widths]
    in_vmem = pl.BlockSpec(memory_space=pltpu.VMEM)
    return pl.pallas_call(
        functools.partial(fused, tuple(widths)),
        out_shape=jax.ShapeDtypeStruct((rows, model), bf16),
        in_specs=[in_vmem] * 5 + [pl.BlockSpec(memory_space=pl.ANY)] * 2,
        out_specs=in_vmem,
        scratch_shapes=scratch,
        compiler_params=pltpu.CompilerParams(
            collective_id=0, has_side_effects=True, vmem_limit_bytes=63 * 1024 * 1024
        ),
        cost_estimate=pl.CostEstimate(
            flops=6 * total * count * half_width * model,
            bytes_accessed=6 * count * half_width * model,
            transcendentals=total * count * half_width,
        ),
    )(
        tokens,
        jnp.transpose(routes),
        jnp.transpose(route_weights),
        bias_gate_up,
        down_bias,
        jnp.transpose(w_gate_up, (0, 2, 3, 1)),
        w_down,
    )


def solution(mesh):
    small = mesh.shape["expert"] == 4 and mesh.shape["tensor"] == 4
    return jax.shard_map(
        fused_local if small else local,
        mesh=mesh,
        in_specs=(
            P(("groups", "expert", "tensor"), None),
            P(("groups", "expert", "tensor"), None),
            P(("groups", "expert", "tensor"), None),
            P("expert", None, None, "tensor"),
            P("expert", None, "tensor"),
            P("expert", "tensor", None),
            P(),
        ),
        out_specs=P(("groups", "expert", "tensor"), None),
        check_vma=False,
    )
```
